256 devices in a mesh: rows: 32 (over y_lo, z, core), chan: 8 (over x, y_hi).
Axes of the slice: x: 4, y: 4 (y_hi: 2, y_lo: 2; y = y_hi * 2 + y_lo), z: 8, core: 2. Of those that a mesh axis runs over, the one named last changes fastest.
Arguments:
- features: bfloat16 [256, 256, 2048], P('rows', None, 'chan'), may hold values from -6 to 6
- grad_out: bfloat16 [3, 256, 256, 256], P(None, 'rows', 'chan'), may hold values from -6 to 6
- pre_act: bfloat16 [3, 256, 256, 256], P(None, 'rows', 'chan'), may hold values from -6 to 6
- weights: bfloat16 [3, 9, 256, 2048], P(None, None, None, 'chan'), may hold values from -0.046875 to 0.046875
Outputs:
- grad_input: bfloat16 [256, 256, 2048], P('rows', None, 'chan')
- grad_weight: float32 [3, 9, 256, 2048], P(None, None, 'rows', 'chan')
The draws below stay inside these ranges and needn't reach their ends.
All inputs are finite; a program needn't handle non-finite values.
Results may differ from the reference program's by a relative error of at most 0.001.
Values may be sent and summed in bfloat16 or wider, within the bound.
A program may use at most 128 MiB of HBM per device.

```python
import jax
import jax.numpy as jnp

C = 2048
COUT = 256
RATE_A = 12
RATE_B = 24
RATE_C = 36
COLS = 256
H = 256


def strengthened(drawn, stream_key, source, target, shards_of, factor):
    owner, partner = [(jnp.arange(drawn.shape[dim]) // (drawn.shape[dim] // shards_of)).reshape([-1 if axis == dim else 1 for axis in range(drawn.ndim)]) for dim in (source, target)]
    chosen = jax.random.permutation(stream_key, shards_of)[partner]
    strong = (owner == chosen) | (owner == (partner + shards_of // 2) % shards_of)
    return jnp.where(strong, factor * drawn, drawn)


def levels(rng, extent, split, low, top_value):
    level = 1.0
    for position, parts in split:
        heights = jax.random.uniform(jax.random.fold_in(jax.random.fold_in(rng, 6), position), (parts,), jnp.float32, low / len(split), top_value / len(split))
        level = level * jnp.repeat(jnp.exp(heights), extent[position] // parts).reshape((-1,) + (1,) * (len(extent) - 1 - position))
    return level


def centred(stream_key, dims, deviation, bound, cuts=(), held_as=jnp.bfloat16):
    entries = deviation * jax.random.normal(stream_key, dims, jnp.float32)
    if cuts:
        entries = entries * levels(stream_key, dims, cuts, -0.22, 0.18)
    return jnp.clip(entries, -bound, bound).astype(held_as)


def noise_with(stream_key, dims, spread, bound, cuts, heavy, dtype=jnp.bfloat16):
    result = spread * jax.random.normal(stream_key, dims, jnp.float32)
    if cuts:
        result = result * levels(stream_key, dims, cuts, -0.22, 0.18)
    return jnp.clip(strengthened(result, jax.random.fold_in(stream_key, 3), *heavy), -bound, bound).astype(dtype)


def setup_inputs(seed: int = 0) -> dict:
    splits = jax.random.split(jax.random.key(seed), 5)
    return {
        "features": centred(splits[0], (H, COLS, C), 1.0, 6.0, ((0, 32), (2, 8))),
        "grad_out": noise_with(splits[1], (3, H, COUT, COLS), 1.0, 6.0, ((1, 32), (2, 8)), (1, 2, 32, 2.75)),
        "pre_act": centred(splits[2], (3, H, COUT, COLS), 1.0, 6.0, ((1, 32), (2, 8))),
        "weights": centred(splits[3], (3, 9, COUT, C), (9 * C) ** -0.5, 0.046875, ((3, 8),)),
    }


grad_scale = 0.00390625


def shifted_field(field, row_step, col_step, dilation):
    padded = jnp.pad(field, ((dilation, dilation), (0, 0), (dilation, dilation)))
    rows_at = dilation - row_step * dilation
    cols_at = dilation - col_step * dilation
    return padded[rows_at:rows_at + H, :, cols_at:cols_at + COLS]


def reference(features, grad_out, pre_act, weights):
    masked = grad_out * (pre_act > 0).astype(jnp.bfloat16)
    feat_wide = features.astype(jnp.float32)
    grad_input = jnp.zeros((H, COLS, C), jnp.float32)
    kernel_list = []
    for branch, dilation in enumerate((RATE_A, RATE_B, RATE_C)):
        tap_list = []
        for row_step in (-1, 0, 1):
            for col_step in (-1, 0, 1):
                tap_index = (row_step + 1) * 3 + (col_step + 1)
                moved = shifted_field(masked[branch], row_step, col_step, dilation).astype(jnp.float32)
                kernel = weights[branch, tap_index].astype(jnp.float32)
                grad_input = grad_input + jnp.einsum('hoc,oi->hci', moved, kernel)
                tap_list.append(jnp.einsum('hoc,hci->oi', moved, feat_wide))
        kernel_list.append(jnp.stack(tap_list, axis=0))
    grad_weight = jnp.stack(kernel_list, axis=0) * grad_scale
    return grad_input.astype(jnp.bfloat16), grad_weight
```

```python
import jax
import jax.numpy as jnp
from jax import lax
from jax.experimental import pallas as pl
from jax.experimental.pallas import tpu as pltpu
from jax.sharding import PartitionSpec as P

RATES = (12, 24, 36)
MESH = pl.DeviceIdType.MESH
BF16 = jnp.bfloat16
F32 = jnp.float32

grad_scale = 0.00390625

PIECES = ((0, 0), (1, 0), (2, 0), (0, -1), (0, 1), (1, -1), (1, 1), (2, -1), (2, 1))
RING = (0, 1, 2, 5, 6, 7, 8)
DIRECT = (3, 4)

STRIP = 8
COLS = 256
UNIT = 32


def row_parts():
    parts = []
    for p, (b, i) in enumerate(PIECES):
        if i == 0:
            continue
        start = -i * RATES[b]
        offset, first = start // STRIP, start % STRIP
        if first == 0:
            parts.append((p, offset, 0, 0, STRIP))
        else:
            parts.append((p, offset, first, 0, STRIP - first))
            parts.append((p, offset + 1, 0, STRIP - first, first))
    return parts


PARTS = row_parts()


def kernel(
    feat, gout, pre, w, gin, gw,
    g, m3, wt, acc, part, r0, qs, ry, sz, rz,
    h_send, h_recv, y_send, y_recv, x_send, x_recv, f_send, f_recv,
    c_send, c_recv, v_send, v_recv, z_send, z_recv,
):
    s = lax.axis_index("rows")
    k = lax.axis_index("chan")
    core = lax.rem(s, 2)
    zpos = lax.rem(s // 2, 8)
    yl = s // 16
    yh = lax.rem(k, 2)
    k_even = k - yh
    k_pair = k + 1 - 2 * yh
    k_left = lax.rem(k + 6, 8)
    k_right = lax.rem(k + 2, 8)

    barrier = pltpu.get_barrier_semaphore()

    @pl.loop(1, 32)
    def _(d):
        pl.semaphore_signal(barrier, inc=1, device_id=(lax.rem(s + d, 32), k), device_id_type=MESH)

    for peer in (k_pair, k_left, k_right):
        pl.semaphore_signal(barrier, inc=1, device_id=(s, peer), device_id_type=MESH)

    own = pl.ds(pl.multiple_of(k * UNIT, UNIT), UNIT)
    for b in range(3):
        for y in range(STRIP):
            value = gout[b, y] * (pre[b, y] > 0).astype(BF16)
            g[b, own, y * COLS : (y + 1) * COLS] = value

    for p, offset, _, here, rows in PARTS:
        @pl.when((s + offset < 0) | (s + offset > 31))
        def _(p=p, here=here, rows=rows):
            cols = slice(here * COLS, (here + rows) * COLS)
            if p in DIRECT:
                g[p, :, cols] = jnp.zeros((256, rows * COLS), BF16)
            else:
                g[p, own, cols] = jnp.zeros((UNIT, rows * COLS), BF16)

    pl.semaphore_wait(barrier, 34)

    def halo_copy(n):
        p, offset, there, here, rows = PARTS[n]
        b = PIECES[p][0]
        take = slice(None) if p in DIRECT else own
        return pltpu.make_async_remote_copy(
            src_ref=g.at[b, take, there * COLS : (there + rows) * COLS],
            dst_ref=g.at[p, take, here * COLS : (here + rows) * COLS],
            send_sem=h_send.at[n], recv_sem=h_recv.at[n],
            device_id=(jnp.clip(s - offset, 0, 31), k), device_id_type=MESH,
        )

    def halo_sends(p):
        for n, entry in enumerate(PARTS):
            if entry[0] == p:
                @pl.when((s - entry[1] >= 0) & (s - entry[1] <= 31))
                def _(n=n):
                    halo_copy(n).start()

    def halo_waits(p):
        for n, entry in enumerate(PARTS):
            if entry[0] == p:
                @pl.when((s + entry[1] >= 0) & (s + entry[1] <= 31))
                def _(n=n):
                    halo_copy(n).wait_recv()

    def halo_drain(p):
        for n, entry in enumerate(PARTS):
            if entry[0] == p:
                @pl.when((s - entry[1] >= 0) & (s - entry[1] <= 31))
                def _(n=n):
                    halo_copy(n).wait_send()

    def remote(src, dst, send, recv, target):
        return pltpu.make_async_remote_copy(
            src_ref=src, dst_ref=dst, send_sem=send, recv_sem=recv, device_id=target, device_id_type=MESH
        )

    def y_copy(p):
        return remote(g.at[p, own], g.at[p, own], y_send.at[p], y_recv.at[p], (s, k_pair))

    def pair_rows(first, count=2 * UNIT):
        return pl.ds(pl.multiple_of(first * UNIT, UNIT), count)

    def x_copies(p):
        rows = pair_rows(k_even)
        return (
            remote(g.at[p, rows], g.at[p, rows], x_send.at[p, 0], x_recv.at[p, 0], (s, k_right)),
            remote(g.at[p, rows], g.at[p, rows], x_send.at[p, 1], x_recv.at[p, 1], (s, k_left)),
        )

    def f_copies(p):
        from_left = pair_rows(lax.rem(k_even + 6, 8), UNIT)
        from_right = pair_rows(lax.rem(k_even + 2, 8) + 1, UNIT)
        return (
            remote(g.at[p, from_left], g.at[p, from_left], f_send.at[p, 0], f_recv.at[p, 0], (s, k_right)),
            remote(g.at[p, from_right], g.at[p, from_right], f_send.at[p, 1], f_recv.at[p, 1], (s, k_left)),
        )

    def stage_y(p):
        if PIECES[p][1] != 0:
            halo_waits(p)
        y_copy(p).start()

    def stage_x(p):
        y_copy(p).wait_recv()
        for copy in x_copies(p):
            copy.start()

    def stage_f(p):
        for copy in x_copies(p):
            copy.wait_recv()
        for copy in f_copies(p):
            copy.start()

    def stage_ready(p):
        if p in DIRECT:
            halo_waits(p)
        else:
            for copy in f_copies(p):
                copy.wait_recv()

    def transpose_kernels(p):
        b, i = PIECES[p]
        for j in range(3):
            wt[p, :, j * 256 : (j + 1) * 256] = w[b, (i + 1) * 3 + j].T

    def c_copy(p):
        return remote(part.at[p, :, :, :, 1 - core], r0.at[p], c_send.at[p], c_recv.at[p], (s + 1 - 2 * core, k))

    def v_copy(p):
        return remote(qs.at[p], ry.at[p], v_send.at[p], v_recv.at[p], (lax.rem(s + 16, 32), k))

    def z_copy(p, d):
        z_to = lax.rem(zpos + d, 8)
        return remote(
            sz.at[p, z_to], rz.at[p, d - 1], z_send.at[p], z_recv.at[p], (yl * 16 + z_to * 2 + core, k)
        )

    def z_whole(p):
        return remote(sz.at[p, 0:7], rz.at[p], z_send.at[p], z_recv.at[p], (lax.rem(s + 2, 32), k))

    def compute(p, first):
        b, i = PIECES[p]
        rate = RATES[b]

        @pl.loop(0, STRIP)
        def _(y):
            cols = pl.ds(pl.multiple_of(y * COLS, COLS), COLS)
            value = g[p, :, cols]
            edge = jnp.zeros((256, rate), BF16)
            m3[0:256, cols] = jnp.concatenate([value[:, rate:], edge], axis=1)
            m3[256:512, cols] = value
            m3[512:768, cols] = jnp.concatenate([edge, value[:, : COLS - rate]], axis=1)

        @pl.loop(0, 3)
        def _(j):
            rows = pl.ds(pl.multiple_of(j * 256, 256), 256)
            product = jnp.dot(m3[rows, :], feat[...], preferred_element_type=F32)
            part[p, j] = product.reshape(2, 8, 2, 8, 256)

        c_copy(p).start()

        @pl.loop(0, STRIP)
        def _(y):
            cols = pl.ds(pl.multiple_of(y * COLS, COLS), COLS)
            product = jnp.dot(wt[p], m3[:, cols], preferred_element_type=F32)
            if first:
                acc[:, cols] = product
            else:
                acc[:, cols] += product

    def reduce_core(p):
        c_copy(p).wait_recv()
        for j in range(3):
            qs[p, j] = part[p, j, 1 - yl, :, core] + r0[p, j, 1 - yl]
        v_copy(p).start()

    def reduce_y(p):
        v_copy(p).wait_recv()
        for j in range(3):
            sz[p, :, j] = part[p, j, yl, :, core] + r0[p, j, yl] + ry[p, j]
        for d in range(1, 8):
            z_copy(p, d).start()

    def reduce_z(p):
        b, i = PIECES[p]
        z_whole(p).wait_recv()
        total = sz[p, zpos]
        for d in range(7):
            total = total + rz[p, d]
        gw[b, 3 * (i + 1) : 3 * (i + 1) + 3] = total * grad_scale

    stage_y(0)
    for p in (1, 2):
        stage_y(p)
    for p in (5, 6, 7, 8):
        halo_sends(p)
    stage_x(0)
    transpose_kernels(0)
    stage_x(1)
    stage_f(0)
    stage_y(5)
    stage_x(2)
    transpose_kernels(1)
    stage_ready(0)
    for p in DIRECT:
        halo_sends(p)
    stage_f(1)
    stage_y(6)
    compute(0, True)
    stage_x(5)
    transpose_kernels(2)
    stage_ready(1)
    stage_f(2)
    stage_y(7)
    compute(1, False)
    reduce_core(0)
    stage_x(6)
    transpose_kernels(3)
    stage_ready(2)
    stage_f(5)
    stage_y(8)
    compute(2, False)
    reduce_core(1)
    reduce_y(0)
    stage_x(7)
    transpose_kernels(5)
    stage_ready(5)
    stage_f(6)
    compute(5, False)
    reduce_core(2)
    reduce_y(1)
    stage_x(8)
    transpose_kernels(4)
    stage_ready(3)
    compute(3, False)
    reduce_core(5)
    reduce_y(2)
    transpose_kernels(6)
    stage_ready(6)
    stage_f(7)
    compute(6, False)
    reduce_core(3)
    reduce_y(5)
    stage_ready(4)
    compute(4, False)
    reduce_core(6)
    reduce_y(3)
    transpose_kernels(7)
    transpose_kernels(8)
    reduce_z(0)
    stage_ready(7)
    stage_f(8)
    compute(7, False)
    reduce_core(4)
    reduce_y(6)
    reduce_z(1)
    reduce_z(2)
    reduce_core(7)
    reduce_y(4)
    stage_ready(8)
    compute(8, False)
    reduce_y(7)
    reduce_core(8)

    @pl.loop(0, STRIP)
    def _(y):
        cols = pl.ds(pl.multiple_of(y * COLS, COLS), COLS)
        gin[y] = acc[:, cols].astype(BF16).T

    reduce_y(8)
    for p in (5, 3, 6, 4, 7, 8):
        reduce_z(p)

    for p in range(9):
        if PIECES[p][1] != 0:
            halo_drain(p)
        if p in RING:
            y_copy(p).wait_send()
            for copy in x_copies(p):
                copy.wait_send()
            for copy in f_copies(p):
                copy.wait_send()
        c_copy(p).wait_send()
        v_copy(p).wait_send()
        z_whole(p).wait_send()


def shards(features, grad_out, pre_act, weights):
    dma = pltpu.SemaphoreType.DMA
    vmem = pl.BlockSpec(memory_space=pltpu.VMEM)
    return pl.pallas_call(
        kernel,
        out_shape=(
            jax.ShapeDtypeStruct((8, 256, 256), BF16),
            jax.ShapeDtypeStruct((3, 9, 8, 256), F32),
        ),
        in_specs=[vmem] * 4,
        out_specs=(vmem, vmem),
        scratch_shapes=[
            pltpu.VMEM((9, 256, 2048), BF16),
            pltpu.VMEM((768, 2048), BF16),
            pltpu.VMEM((9, 256, 768), BF16),
            pltpu.VMEM((256, 2048), F32),
            pltpu.VMEM((9, 3, 2, 8, 2, 8, 256), F32),
            pltpu.VMEM((9, 3, 2, 8, 8, 256), F32),
            pltpu.VMEM((9, 3, 8, 8, 256), F32),
            pltpu.VMEM((9, 3, 8, 8, 256), F32),
            pltpu.VMEM((9, 8, 3, 8, 256), F32),
            pltpu.VMEM((9, 7, 3, 8, 256), F32),
            dma((len(PARTS),)), dma((len(PARTS),)),
            dma((9,)), dma((9,)),
            dma((9, 2)), dma((9, 2)),
            dma((9, 2)), dma((9, 2)),
            dma((9,)), dma((9,)),
            dma((9,)), dma((9,)),
            dma((9,)), dma((9,)),
        ],
        compiler_params=pltpu.CompilerParams(
            collective_id=0, has_side_effects=True, vmem_limit_bytes=62 * 2**20
        ),
        cost_estimate=pl.CostEstimate(flops=14495514624, bytes_accessed=8 * 2**20, transcendentals=0),
    )(features.reshape(2048, 256), grad_out, pre_act, weights)


def solution(mesh):
    in_specs = (
        P("rows", None, "chan"),
        P(None, "rows", "chan", None),
        P(None, "rows", "chan", None),
        P(None, None, None, "chan"),
    )
    out_specs = (P("rows", None, "chan"), P(None, None, "rows", "chan"))
    return jax.shard_map(shards, mesh=mesh, in_specs=in_specs, out_specs=out_specs, check_vma=False)
```

```python
import jax
import jax.numpy as jnp
from jax import lax
from jax.experimental import pallas as pl
from jax.experimental.pallas import tpu as pltpu
from jax.sharding import PartitionSpec as P

RATES = (12, 24, 36)
MESH = pl.DeviceIdType.MESH
BF16 = jnp.bfloat16
F32 = jnp.float32

grad_scale = 0.00390625

PIECES = ((0, 0), (1, 0), (2, 0), (0, -1), (0, 1), (1, -1), (1, 1), (2, -1), (2, 1))
RING = (0, 1, 2, 5, 6, 7, 8)
DIRECT = (3, 4)

STRIP = 8
COLS = 256
UNIT = 32


def row_parts():
    parts = []
    for p, (b, i) in enumerate(PIECES):
        if i == 0:
            continue
        start = -i * RATES[b]
        offset, first = start // STRIP, start % STRIP
        if first == 0:
            parts.append((p, offset, 0, 0, STRIP))
        else:
            parts.append((p, offset, first, 0, STRIP - first))
            parts.append((p, offset + 1, 0, STRIP - first, first))
    return parts


PARTS = row_parts()


def kernel(
    feat, gout, pre, w_hbm, gin, gw,
    w, g, m3, wt, acc, part, r0, qs, ry, sz, rz,
    h_send, h_recv, y_send, y_recv, x_send, x_recv, f_send, f_recv,
    c_send, c_recv, v_send, v_recv, z_send, z_recv, e_send, e_recv, w_sem,
):
    s = lax.axis_index("rows")
    k = lax.axis_index("chan")
    core = lax.rem(s, 2)
    zpos = lax.rem(s // 2, 8)
    yl = s // 16
    yh = lax.rem(k, 2)
    k_even = k - yh
    k_pair = k + 1 - 2 * yh
    k_left = lax.rem(k + 6, 8)
    k_right = lax.rem(k + 2, 8)

    w_copy = pltpu.make_async_copy(w_hbm, w, w_sem)
    w_copy.start()
    barrier = pltpu.get_barrier_semaphore()

    for d in (1, 2, 3, 4, 5):
        for side in (d, 32 - d):
            pl.semaphore_signal(barrier, inc=1, device_id=(lax.rem(s + side, 32), k), device_id_type=MESH)
    for d in range(1, 8):
        z_peer = yl * 16 + lax.rem(zpos + d, 8) * 2 + core
        pl.semaphore_signal(barrier, inc=1, device_id=(z_peer, k), device_id_type=MESH)
    pl.semaphore_signal(barrier, inc=1, device_id=(lax.rem(s + 16, 32), k), device_id_type=MESH)
    for peer in (k_pair, k_left, k_right):
        pl.semaphore_signal(barrier, inc=1, device_id=(s, peer), device_id_type=MESH)

    own = pl.ds(pl.multiple_of(k * UNIT, UNIT), UNIT)
    for b in range(3):
        for y in range(STRIP):
            value = gout[b, y] * (pre[b, y] > 0).astype(BF16)
            g[b, own, y * COLS : (y + 1) * COLS] = value

    for p, offset, _, here, rows in PARTS:
        @pl.when((s + offset < 0) | (s + offset > 31))
        def _(p=p, here=here, rows=rows):
            cols = slice(here * COLS, (here + rows) * COLS)
            if p in DIRECT:
                g[p, :, cols] = jnp.zeros((256, rows * COLS), BF16)
            else:
                g[p, own, cols] = jnp.zeros((UNIT, rows * COLS), BF16)

    pl.semaphore_wait(barrier, 21)

    def halo_copy(n):
        p, offset, there, here, rows = PARTS[n]
        b = PIECES[p][0]
        take = slice(None) if p in DIRECT else own
        return pltpu.make_async_remote_copy(
            src_ref=g.at[b, take, there * COLS : (there + rows) * COLS],
            dst_ref=g.at[p, take, here * COLS : (here + rows) * COLS],
            send_sem=h_send.at[n], recv_sem=h_recv.at[n],
            device_id=(jnp.clip(s - offset, 0, 31), k), device_id_type=MESH,
        )

    def halo_sends(p):
        for n, entry in enumerate(PARTS):
            if entry[0] == p:
                @pl.when((s - entry[1] >= 0) & (s - entry[1] <= 31))
                def _(n=n):
                    halo_copy(n).start()

    def halo_waits(p):
        for n, entry in enumerate(PARTS):
            if entry[0] == p:
                @pl.when((s + entry[1] >= 0) & (s + entry[1] <= 31))
                def _(n=n):
                    halo_copy(n).wait_recv()

    def halo_drain(p):
        for n, entry in enumerate(PARTS):
            if entry[0] == p:
                @pl.when((s - entry[1] >= 0) & (s - entry[1] <= 31))
                def _(n=n):
                    halo_copy(n).wait_send()

    def remote(src, dst, send, recv, target):
        return pltpu.make_async_remote_copy(
            src_ref=src, dst_ref=dst, send_sem=send, recv_sem=recv, device_id=target, device_id_type=MESH
        )

    def y_copy(p):
        return remote(g.at[p, own], g.at[p, own], y_send.at[p], y_recv.at[p], (s, k_pair))

    def pair_rows(first, count=2 * UNIT):
        return pl.ds(pl.multiple_of(first * UNIT, UNIT), count)

    def e_copies():
        return (
            remote(g.at[0, own], g.at[0, own], e_send.at[0], e_recv.at[0], (s, k_right)),
            remote(g.at[0, own], g.at[0, own], e_send.at[1], e_recv.at[1], (s, k_left)),
        )

    def x_copies(p):
        rows = pair_rows(k_pair, UNIT) if p == 0 else pair_rows(k_even)
        return (
            remote(g.at[p, rows], g.at[p, rows], x_send.at[p, 0], x_recv.at[p, 0], (s, k_right)),
            remote(g.at[p, rows], g.at[p, rows], x_send.at[p, 1], x_recv.at[p, 1], (s, k_left)),
        )

    def f_copies(p):
        from_left = pair_rows(lax.rem(k_even + 6, 8), UNIT)
        from_right = pair_rows(lax.rem(k_even + 2, 8) + 1, UNIT)
        return (
            remote(g.at[p, from_left], g.at[p, from_left], f_send.at[p, 0], f_recv.at[p, 0], (s, k_right)),
            remote(g.at[p, from_right], g.at[p, from_right], f_send.at[p, 1], f_recv.at[p, 1], (s, k_left)),
        )

    def stage_y(p):
        if PIECES[p][1] != 0:
            halo_waits(p)
        y_copy(p).start()

    def stage_x(p):
        y_copy(p).wait_recv()
        for copy in x_copies(p):
            copy.start()

    def stage_f(p):
        if p == 0:
            for copy in e_copies():
                copy.wait_recv()
        for copy in x_copies(p):
            copy.wait_recv()
        for copy in f_copies(p):
            copy.start()

    def stage_ready(p):
        if p in DIRECT:
            halo_waits(p)
        else:
            for copy in f_copies(p):
                copy.wait_recv()

    def transpose_kernels(p):
        b, i = PIECES[p]
        for j in range(3):
            wt[p, :, j * 256 : (j + 1) * 256] = w[b, (i + 1) * 3 + j].T

    def c_copy(p):
        return remote(part.at[p, :, :, :, 1 - core], r0.at[p], c_send.at[p], c_recv.at[p], (s + 1 - 2 * core, k))

    def v_copy(p):
        return remote(qs.at[p], ry.at[p], v_send.at[p], v_recv.at[p], (lax.rem(s + 16, 32), k))

    def z_copy(p, d):
        z_to = lax.rem(zpos + d, 8)
        return remote(
            sz.at[p, z_to], rz.at[p, d - 1], z_send.at[p], z_recv.at[p], (yl * 16 + z_to * 2 + core, k)
        )

    def z_whole(p):
        return remote(sz.at[p, 0:7], rz.at[p], z_send.at[p], z_recv.at[p], (lax.rem(s + 2, 32), k))

    def compute(p, first):
        b, i = PIECES[p]
        rate = RATES[b]

        lane = lax.broadcasted_iota(jnp.int32, (1, COLS), 1)
        keep_lo = (lane >= rate).astype(F32).astype(BF16)
        keep_hi = (lane < COLS - rate).astype(F32).astype(BF16)
        for y in range(STRIP):
            cols = slice(y * COLS, (y + 1) * COLS)
            value = g[p, :, cols]
            m3[0:256, cols] = pltpu.roll(value, COLS - rate, 1) * keep_hi
            m3[256:512, cols] = value
            m3[512:768, cols] = pltpu.roll(value, rate, 1) * keep_lo

        product = jnp.dot(m3[...], feat[...], preferred_element_type=F32)
        part[p] = product.reshape(3, 2, 8, 2, 8, 256)

        c_copy(p).start()

        for h in range(2):
            cols = slice(h * 1024, (h + 1) * 1024)
            product = jnp.dot(wt[p], m3[:, cols], preferred_element_type=F32)
            if first:
                acc[:, cols] = product
            else:
                acc[:, cols] += product

    def reduce_core(p):
        c_copy(p).wait_recv()
        for j in range(3):
            qs[p, j] = part[p, j, 1 - yl, :, core] + r0[p, j, 1 - yl]
        v_copy(p).start()

    def reduce_y(p):
        v_copy(p).wait_recv()
        for j in range(3):
            sz[p, :, j] = part[p, j, yl, :, core] + r0[p, j, yl] + ry[p, j]
        for d in range(1, 8):
            z_copy(p, d).start()

    def reduce_z(p):
        b, i = PIECES[p]
        z_whole(p).wait_recv()
        total = sz[p, zpos]
        for d in range(7):
            total = total + rz[p, d]
        gw[b, 3 * (i + 1) : 3 * (i + 1) + 3] = total * grad_scale

    stage_y(0)
    for copy in e_copies():
        copy.start()
    for p in (1, 2):
        stage_y(p)
    for p in (5, 6, 7, 8):
        halo_sends(p)
    stage_x(0)
    w_copy.wait()
    transpose_kernels(0)
    stage_x(1)
    stage_f(0)
    stage_y(5)
    stage_x(2)
    transpose_kernels(1)
    stage_ready(0)
    for p in DIRECT:
        halo_sends(p)
    stage_f(1)
    stage_y(6)
    compute(0, True)
    stage_x(5)
    transpose_kernels(2)
    reduce_core(0)
    stage_ready(1)
    stage_f(2)
    stage_y(7)
    compute(1, False)
    stage_x(6)
    transpose_kernels(3)
    reduce_core(1)
    reduce_y(0)
    stage_ready(2)
    stage_f(5)
    stage_y(8)
    compute(2, False)
    stage_x(7)
    transpose_kernels(4)
    reduce_core(2)
    reduce_y(1)
    stage_ready(3)
    compute(3, False)
    transpose_kernels(5)
    stage_ready(5)
    stage_f(6)
    compute(5, False)
    stage_x(8)
    reduce_core(3)
    reduce_y(2)
    stage_ready(4)
    compute(4, False)
    transpose_kernels(6)
    reduce_core(5)
    reduce_y(3)
    stage_ready(6)
    stage_f(7)
    compute(6, False)
    reduce_core(4)
    reduce_y(5)
    transpose_kernels(7)
    transpose_kernels(8)
    stage_ready(7)
    stage_f(8)
    compute(7, False)
    reduce_core(6)
    reduce_y(4)
    reduce_core(7)
    reduce_y(6)
    for p in (0, 1, 2, 3):
        reduce_z(p)
    stage_ready(8)
    compute(8, False)
    reduce_y(7)
    reduce_core(8)

    @pl.loop(0, STRIP)
    def _(y):
        cols = pl.ds(pl.multiple_of(y * COLS, COLS), COLS)
        gin[y] = acc[:, cols].astype(BF16).T

    reduce_y(8)
    for p in (5, 4, 6, 7, 8):
        reduce_z(p)

    for copy in e_copies():
        copy.wait_send()
    for p in range(9):
        if PIECES[p][1] != 0:
            halo_drain(p)
        if p in RING:
            y_copy(p).wait_send()
            for copy in x_copies(p):
                copy.wait_send()
            for copy in f_copies(p):
                copy.wait_send()
        c_copy(p).wait_send()
        v_copy(p).wait_send()
        z_whole(p).wait_send()


def shards(features, grad_out, pre_act, weights):
    dma = pltpu.SemaphoreType.DMA
    vmem = pl.BlockSpec(memory_space=pltpu.VMEM)
    return pl.pallas_call(
        kernel,
        out_shape=(
            jax.ShapeDtypeStruct((8, 256, 256), BF16),
            jax.ShapeDtypeStruct((3, 9, 8, 256), F32),
        ),
        in_specs=[vmem] * 3 + [pl.BlockSpec(memory_space=pl.ANY)],
        out_specs=(vmem, vmem),
        scratch_shapes=[
            pltpu.VMEM((3, 9, 256, 256), BF16),
            pltpu.VMEM((9, 256, 2048), BF16),
            pltpu.VMEM((768, 2048), BF16),
            pltpu.VMEM((9, 256, 768), BF16),
            pltpu.VMEM((256, 2048), F32),
            pltpu.VMEM((9, 3, 2, 8, 2, 8, 256), F32),
            pltpu.VMEM((9, 3, 2, 8, 8, 256), F32),
            pltpu.VMEM((9, 3, 8, 8, 256), F32),
            pltpu.VMEM((9, 3, 8, 8, 256), F32),
            pltpu.VMEM((9, 8, 3, 8, 256), F32),
            pltpu.VMEM((9, 7, 3, 8, 256), F32),
            dma((len(PARTS),)), dma((len(PARTS),)),
            dma((9,)), dma((9,)),
            dma((9, 2)), dma((9, 2)),
            dma((9, 2)), dma((9, 2)),
            dma((9,)), dma((9,)),
            dma((9,)), dma((9,)),
            dma((9,)), dma((9,)),
            dma((2,)), dma((2,)),
            pltpu.SemaphoreType.DMA,
        ],
        compiler_params=pltpu.CompilerParams(
            collective_id=0, has_side_effects=True, vmem_limit_bytes=62 * 2**20
        ),
        cost_estimate=pl.CostEstimate(flops=14495514624, bytes_accessed=8 * 2**20, transcendentals=0),
    )(features.reshape(2048, 256), grad_out, pre_act, weights)


def solution(mesh):
    in_specs = (
        P("rows", None, "chan"),
        P(None, "rows", "chan", None),
        P(None, "rows", "chan", None),
        P(None, None, None, "chan"),
    )
    out_specs = (P("rows", None, "chan"), P(None, None, "rows", "chan"))
    return jax.shard_map(shards, mesh=mesh, in_specs=in_specs, out_specs=out_specs, check_vma=False)
```

```python
import jax
import jax.numpy as jnp
from jax import lax
from jax.experimental import pallas as pl
from jax.experimental.pallas import tpu as pltpu
from jax.sharding import PartitionSpec as P

RATES = (12, 24, 36)
MESH = pl.DeviceIdType.MESH
BF16 = jnp.bfloat16
F32 = jnp.float32

grad_scale = 0.00390625

PIECES = ((0, 0), (1, 0), (2, 0), (0, -1), (0, 1), (1, -1), (1, 1), (2, -1), (2, 1))
RING = (0, 1, 2, 5, 6, 7, 8)
DIRECT = (3, 4)

STRIP = 8
COLS = 256
SPLIT = (8,)
UNIT = 32


ORDER = (
    "y0", "e0", "y1", "y2", "h5", "h6", "h7", "h8", "x0", "w0", "t0", "x1",
    "f0", "y5", "x2", "t1", "r0", "h3", "h4", "f1", "y6", "k0", "I0", "x5",
    "t2", "c0", "r1", "f2", "y7", "k1", "i1", "x6", "t3", "c1", "r2", "f5",
    "y8", "k2", "i2", "x7", "t4", "c2", "v0", "r3", "k3", "i3", "t5", "r5",
    "f6", "k5", "i5", "x8", "c3", "v1", "r4", "k4", "i4", "t6", "c5", "v2",
    "r6", "f7", "k6", "i6", "c4", "v3", "t7", "t8", "r7", "f8", "k7", "i7",
    "v5", "c6", "c7", "v4", "z0", "z1", "r8", "k8", "C8", "v6", "v7", "i8",
    "V8", "o0", "z2", "z3", "z5", "z4", "z6", "z7", "z8",
)


def row_parts():
    parts = []
    for p, (b, i) in enumerate(PIECES):
        if i == 0:
            continue
        start = -i * RATES[b]
        offset, first = start // STRIP, start % STRIP
        if first == 0:
            parts.append((p, offset, 0, 0, STRIP))
        else:
            parts.append((p, offset, first, 0, STRIP - first))
            parts.append((p, offset + 1, 0, STRIP - first, first))
    return parts


PARTS = row_parts()


def chunks(p):
    return (0, 1, 2) if p in SPLIT else (None,)


def kernel(
    feat, gout, pre, w_hbm, gin, gw,
    w, g, m3, wt, acc, part, r0, qs, ry, sz, rz,
    h_send, h_recv, y_send, y_recv, x_send, x_recv, f_send, f_recv,
    c_send, c_recv, v_send, v_recv, z_send, z_recv, e_send, e_recv, w_sem,
):
    s = lax.axis_index("rows")
    k = lax.axis_index("chan")
    core = lax.rem(s, 2)
    zpos = lax.rem(s // 2, 8)
    yl = s // 16
    yh = lax.rem(k, 2)
    k_even = k - yh
    k_pair = k + 1 - 2 * yh
    k_left = lax.rem(k + 6, 8)
    k_right = lax.rem(k + 2, 8)

    w_copy = pltpu.make_async_copy(w_hbm, w, w_sem)
    w_copy.start()
    barrier = pltpu.get_barrier_semaphore()

    for d in (1, 2, 3, 4, 5):
        for side in (d, 32 - d):
            pl.semaphore_signal(barrier, inc=1, device_id=(lax.rem(s + side, 32), k), device_id_type=MESH)
    for d in range(1, 8):
        z_peer = yl * 16 + lax.rem(zpos + d, 8) * 2 + core
        pl.semaphore_signal(barrier, inc=1, device_id=(z_peer, k), device_id_type=MESH)
    pl.semaphore_signal(barrier, inc=1, device_id=(lax.rem(s + 16, 32), k), device_id_type=MESH)
    for peer in (k_pair, k_left, k_right):
        pl.semaphore_signal(barrier, inc=1, device_id=(s, peer), device_id_type=MESH)

    own = pl.ds(pl.multiple_of(k * UNIT, UNIT), UNIT)
    for b in range(3):
        for y in range(STRIP):
            value = gout[b, y] * (pre[b, y] > 0).astype(BF16)
            g[b, own, y * COLS : (y + 1) * COLS] = value

    for p, offset, _, here, rows in PARTS:
        @pl.when((s + offset < 0) | (s + offset > 31))
        def _(p=p, here=here, rows=rows):
            cols = slice(here * COLS, (here + rows) * COLS)
            if p in DIRECT:
                g[p, :, cols] = jnp.zeros((256, rows * COLS), BF16)
            else:
                g[p, own, cols] = jnp.zeros((UNIT, rows * COLS), BF16)

    pl.semaphore_wait(barrier, 21)

    def halo_copy(n):
        p, offset, there, here, rows = PARTS[n]
        b = PIECES[p][0]
        take = slice(None) if p in DIRECT else own
        return pltpu.make_async_remote_copy(
            src_ref=g.at[b, take, there * COLS : (there + rows) * COLS],
            dst_ref=g.at[p, take, here * COLS : (here + rows) * COLS],
            send_sem=h_send.at[n], recv_sem=h_recv.at[n],
            device_id=(jnp.clip(s - offset, 0, 31), k), device_id_type=MESH,
        )

    def halo_sends(p):
        for n, entry in enumerate(PARTS):
            if entry[0] == p:
                @pl.when((s - entry[1] >= 0) & (s - entry[1] <= 31))
                def _(n=n):
                    halo_copy(n).start()

    def halo_waits(p):
        for n, entry in enumerate(PARTS):
            if entry[0] == p:
                @pl.when((s + entry[1] >= 0) & (s + entry[1] <= 31))
                def _(n=n):
                    halo_copy(n).wait_recv()

    def halo_drain(p):
        for n, entry in enumerate(PARTS):
            if entry[0] == p:
                @pl.when((s - entry[1] >= 0) & (s - entry[1] <= 31))
                def _(n=n):
                    halo_copy(n).wait_send()

    def remote(src, dst, send, recv, target):
        return pltpu.make_async_remote_copy(
            src_ref=src, dst_ref=dst, send_sem=send, recv_sem=recv, device_id=target, device_id_type=MESH
        )

    def y_copy(p):
        return remote(g.at[p, own], g.at[p, own], y_send.at[p], y_recv.at[p], (s, k_pair))

    def pair_rows(first, count=2 * UNIT):
        return pl.ds(pl.multiple_of(first * UNIT, UNIT), count)

    def e_copies():
        return (
            remote(g.at[0, own], g.at[0, own], e_send.at[0], e_recv.at[0], (s, k_right)),
            remote(g.at[0, own], g.at[0, own], e_send.at[1], e_recv.at[1], (s, k_left)),
        )

    def x_copies(p):
        rows = pair_rows(k_pair, UNIT) if p == 0 else pair_rows(k_even)
        return (
            remote(g.at[p, rows], g.at[p, rows], x_send.at[p, 0], x_recv.at[p, 0], (s, k_right)),
            remote(g.at[p, rows], g.at[p, rows], x_send.at[p, 1], x_recv.at[p, 1], (s, k_left)),
        )

    def f_copies(p):
        from_left = pair_rows(lax.rem(k_even + 6, 8), UNIT)
        from_right = pair_rows(lax.rem(k_even + 2, 8) + 1, UNIT)
        return (
            remote(g.at[p, from_left], g.at[p, from_left], f_send.at[p, 0], f_recv.at[p, 0], (s, k_right)),
            remote(g.at[p, from_right], g.at[p, from_right], f_send.at[p, 1], f_recv.at[p, 1], (s, k_left)),
        )

    def stage_y(p):
        if PIECES[p][1] != 0:
            halo_waits(p)
        y_copy(p).start()

    def stage_x(p):
        y_copy(p).wait_recv()
        for copy in x_copies(p):
            copy.start()

    def stage_f(p):
        if p == 0:
            for copy in e_copies():
                copy.wait_recv()
        for copy in x_copies(p):
            copy.wait_recv()
        for copy in f_copies(p):
            copy.start()

    def stage_ready(p):
        if p in DIRECT:
            halo_waits(p)
        else:
            for copy in f_copies(p):
                copy.wait_recv()

    def transpose_kernels(p):
        b, i = PIECES[p]
        for j in range(3):
            wt[p, :, j * 256 : (j + 1) * 256] = w[b, (i + 1) * 3 + j].T

    def slot(p, j):
        return p if j is None else p + j

    def c_copy(p, j=None):
        src, dst = (part.at[p], r0.at[p]) if j is None else (part.at[p, j : j + 1], r0.at[p, j : j + 1])
        n = slot(p, j)
        return remote(src.at[:, :, :, 1 - core], dst, c_send.at[n], c_recv.at[n], (s + 1 - 2 * core, k))

    def v_copy(p, j=None):
        src, dst = (qs.at[p], ry.at[p]) if j is None else (qs.at[p, j], ry.at[p, j])
        n = slot(p, j)
        return remote(src, dst, v_send.at[n], v_recv.at[n], (lax.rem(s + 16, 32), k))

    def z_copy(p, d, j=None):
        z_to = lax.rem(zpos + d, 8)
        src, dst = sz.at[p, z_to], rz.at[p, d - 1]
        if j is not None:
            src, dst = src.at[j], dst.at[j]
        n = slot(p, j)
        return remote(src, dst, z_send.at[n], z_recv.at[n], (yl * 16 + z_to * 2 + core, k))

    def z_whole(p, j=None):
        src, dst = sz.at[p, 0:7], rz.at[p]
        if j is not None:
            src, dst = src.at[:, j], dst.at[:, j]
        n = slot(p, j)
        return remote(src, dst, z_send.at[n], z_recv.at[n], (lax.rem(s + 2, 32), k))

    def compute_kernels(p):
        b, i = PIECES[p]
        rate = RATES[b]

        lane = lax.broadcasted_iota(jnp.int32, (1, COLS), 1)
        keep_lo = (lane >= rate).astype(F32).astype(BF16)
        keep_hi = (lane < COLS - rate).astype(F32).astype(BF16)
        for y in range(STRIP):
            cols = slice(y * COLS, (y + 1) * COLS)
            value = g[p, :, cols]
            m3[0:256, cols] = pltpu.roll(value, COLS - rate, 1) * keep_hi
            m3[256:512, cols] = value
            m3[512:768, cols] = pltpu.roll(value, rate, 1) * keep_lo

        if p in SPLIT:
            for j in range(3):
                product = jnp.dot(m3[j * 256 : (j + 1) * 256, :], feat[...], preferred_element_type=F32)
                part[p, j] = product.reshape(2, 8, 2, 8, 256)
                c_copy(p, j).start()
        else:
            product = jnp.dot(m3[...], feat[...], preferred_element_type=F32)
            part[p] = product.reshape(3, 2, 8, 2, 8, 256)
            c_copy(p).start()

    def compute_input(p, first=False):
        for h in range(2):
            cols = slice(h * 1024, (h + 1) * 1024)
            product = jnp.dot(wt[p], m3[:, cols], preferred_element_type=F32)
            if first:
                acc[:, cols] = product
            else:
                acc[:, cols] += product

    def compute(p, first=False):
        compute_kernels(p)
        compute_input(p, first)

    def reduce_core(p, only=None):
        c_copy(p, only).wait_recv()
        for j in range(3) if only is None else (only,):
            qs[p, j] = part[p, j, 1 - yl, :, core] + r0[p, j, 1 - yl]
        v_copy(p, only).start()

    def reduce_y(p, only=None):
        v_copy(p, only).wait_recv()
        for j in range(3) if only is None else (only,):
            sz[p, :, j] = part[p, j, yl, :, core] + r0[p, j, yl] + ry[p, j]
        for d in range(1, 8):
            z_copy(p, d, only).start()

    def reduce_z(p):
        b, i = PIECES[p]
        for only in chunks(p):
            z_whole(p, only).wait_recv()
        total = sz[p, zpos]
        for d in range(7):
            total = total + rz[p, d]
        gw[b, 3 * (i + 1) : 3 * (i + 1) + 3] = total * grad_scale

    def own_first(_):
        for copy in e_copies():
            copy.start()

    def weights_in(_):
        w_copy.wait()

    def split_core(p):
        for j in range(3):
            reduce_core(p, j)

    def split_y(p):
        for j in range(3):
            reduce_y(p, j)

    def write_input(_):
        for y in range(STRIP):
            gin[y] = acc[:, y * COLS : (y + 1) * COLS].astype(BF16).T

    steps = {
        "e": own_first, "y": stage_y, "h": halo_sends, "x": stage_x, "f": stage_f, "r": stage_ready,
        "w": weights_in, "t": transpose_kernels, "k": compute_kernels, "i": compute_input,
        "I": lambda p: compute_input(p, True), "c": reduce_core, "v": reduce_y, "z": reduce_z,
        "C": split_core, "V": split_y, "o": write_input,
    }
    for step in ORDER:
        steps[step[0]](int(step[1]))

    for copy in e_copies():
        copy.wait_send()
    for p in range(9):
        if PIECES[p][1] != 0:
            halo_drain(p)
        if p in RING:
            y_copy(p).wait_send()
            for copy in x_copies(p):
                copy.wait_send()
            for copy in f_copies(p):
                copy.wait_send()
        for j in chunks(p):
            c_copy(p, j).wait_send()
            v_copy(p, j).wait_send()
            z_whole(p, j).wait_send()


def shards(features, grad_out, pre_act, weights):
    dma = pltpu.SemaphoreType.DMA
    vmem = pl.BlockSpec(memory_space=pltpu.VMEM)
    return pl.pallas_call(
        kernel,
        out_shape=(
            jax.ShapeDtypeStruct((8, 256, 256), BF16),
            jax.ShapeDtypeStruct((3, 9, 8, 256), F32),
        ),
        in_specs=[vmem] * 3 + [pl.BlockSpec(memory_space=pl.ANY)],
        out_specs=(vmem, vmem),
        scratch_shapes=[
            pltpu.VMEM((3, 9, 256, 256), BF16),
            pltpu.VMEM((9, 256, 2048), BF16),
            pltpu.VMEM((768, 2048), BF16),
            pltpu.VMEM((9, 256, 768), BF16),
            pltpu.VMEM((256, 2048), F32),
            pltpu.VMEM((9, 3, 2, 8, 2, 8, 256), F32),
            pltpu.VMEM((9, 3, 2, 8, 8, 256), F32),
            pltpu.VMEM((9, 3, 8, 8, 256), F32),
            pltpu.VMEM((9, 3, 8, 8, 256), F32),
            pltpu.VMEM((9, 8, 3, 8, 256), F32),
            pltpu.VMEM((9, 7, 3, 8, 256), F32),
            dma((len(PARTS),)), dma((len(PARTS),)),
            dma((9,)), dma((9,)),
            dma((9, 2)), dma((9, 2)),
            dma((9, 2)), dma((9, 2)),
            dma((11,)), dma((11,)),
            dma((11,)), dma((11,)),
            dma((11,)), dma((11,)),
            dma((2,)), dma((2,)),
            pltpu.SemaphoreType.DMA,
        ],
        compiler_params=pltpu.CompilerParams(
            collective_id=0, has_side_effects=True, vmem_limit_bytes=62 * 2**20
        ),
        cost_estimate=pl.CostEstimate(flops=14495514624, bytes_accessed=8 * 2**20, transcendentals=0),
    )(features.reshape(2048, 256), grad_out, pre_act, weights)


def solution(mesh):
    in_specs = (
        P("rows", None, "chan"),
        P(None, "rows", "chan", None),
        P(None, "rows", "chan", None),
        P(None, None, None, "chan"),
    )
    out_specs = (P("rows", None, "chan"), P(None, None, "rows", "chan"))
    return jax.shard_map(shards, mesh=mesh, in_specs=in_specs, out_specs=out_specs, check_vma=False)
```

```python
import jax
import jax.numpy as jnp
from jax import lax
from jax.experimental import pallas as pl
from jax.experimental.pallas import tpu as pltpu
from jax.sharding import PartitionSpec as P

RATES = (12, 24, 36)
MESH = pl.DeviceIdType.MESH
BF16 = jnp.bfloat16
F32 = jnp.float32

grad_scale = 0.00390625

PIECES = ((0, 0), (1, 0), (2, 0), (0, -1), (0, 1), (1, -1), (1, 1), (2, -1), (2, 1))
RING = (0, 1, 2, 5, 6, 7, 8)
DIRECT = (3, 4)

STRIP = 8
COLS = 256
SPLIT = (8,)
UNIT = 32


ORDER = (
    "y0", "e0", "y1", "y2", "h5", "h6", "h7", "h8", "x0", "w0", "t0", "x1",
    "f0", "y5", "x2", "t1", "r0", "h3", "h4", "f1", "y6", "k0", "I0", "x5",
    "t2", "c0", "r1", "f2", "y7", "k1", "i1", "x6", "t3", "c1", "r2", "f5",
    "y8", "k2", "i2", "x7", "t4", "c2", "v0", "r3", "k3", "i3", "t5", "r5",
    "f6", "k5", "i5", "x8", "c3", "v1", "r4", "k4", "i4", "t6", "c5", "v2",
    "r6", "f7", "k6", "i6", "c4", "v3", "t7", "t8", "r7", "f8", "k7", "i7",
    "v5", "c6", "c7", "v4", "z0", "z1", "r8", "k8", "C8", "v6", "v7", "i8",
    "V8", "o0", "z2", "z3", "z5", "z4", "z6", "z7", "z8",
)


def row_parts():
    parts = []
    for p, (b, i) in enumerate(PIECES):
        if i == 0:
            continue
        start = -i * RATES[b]
        offset, first = start // STRIP, start % STRIP
        if first == 0:
            parts.append((p, offset, 0, 0, STRIP))
        else:
            parts.append((p, offset, first, 0, STRIP - first))
            parts.append((p, offset + 1, 0, STRIP - first, first))
    return parts


PARTS = row_parts()


def chunks(p):
    return (0, 1, 2) if p in SPLIT else (None,)


def kernel(
    feat_hbm, gout, pre, w_hbm, gin, gw,
    feat, w, g, m3, wt, acc, part, r0, qs, ry, sz, rz,
    h_send, h_recv, y_send, y_recv, x_send, x_recv, f_send, f_recv,
    c_send, c_recv, v_send, v_recv, z_send, z_recv, e_send, e_recv, w_sem, feat_sem,
):
    s = lax.axis_index("rows")
    k = lax.axis_index("chan")
    core = lax.rem(s, 2)
    zpos = lax.rem(s // 2, 8)
    yl = s // 16
    yh = lax.rem(k, 2)
    k_even = k - yh
    k_pair = k + 1 - 2 * yh
    k_left = lax.rem(k + 6, 8)
    k_right = lax.rem(k + 2, 8)

    w_copy = pltpu.make_async_copy(w_hbm, w, w_sem)
    w_copy.start()
    feat_copy = pltpu.make_async_copy(feat_hbm, feat, feat_sem)
    feat_copy.start()
    barrier = pltpu.get_barrier_semaphore()

    for d in (1, 2, 3, 4, 5):
        for side in (d, 32 - d):
            pl.semaphore_signal(barrier, inc=1, device_id=(lax.rem(s + side, 32), k), device_id_type=MESH)
    for d in range(1, 8):
        z_peer = yl * 16 + lax.rem(zpos + d, 8) * 2 + core
        pl.semaphore_signal(barrier, inc=1, device_id=(z_peer, k), device_id_type=MESH)
    pl.semaphore_signal(barrier, inc=1, device_id=(lax.rem(s + 16, 32), k), device_id_type=MESH)
    for peer in (k_pair, k_left, k_right):
        pl.semaphore_signal(barrier, inc=1, device_id=(s, peer), device_id_type=MESH)

    own = pl.ds(pl.multiple_of(k * UNIT, UNIT), UNIT)
    for b in range(3):
        for y in range(STRIP):
            value = gout[b, y] * (pre[b, y] > 0).astype(BF16)
            g[b, own, y * COLS : (y + 1) * COLS] = value

    for p, offset, _, here, rows in PARTS:
        @pl.when((s + offset < 0) | (s + offset > 31))
        def _(p=p, here=here, rows=rows):
            cols = slice(here * COLS, (here + rows) * COLS)
            if p in DIRECT:
                g[p, :, cols] = jnp.zeros((256, rows * COLS), BF16)
            else:
                g[p, own, cols] = jnp.zeros((UNIT, rows * COLS), BF16)

    pl.semaphore_wait(barrier, 21)

    def halo_copy(n):
        p, offset, there, here, rows = PARTS[n]
        b = PIECES[p][0]
        take = slice(None) if p in DIRECT else own
        return pltpu.make_async_remote_copy(
            src_ref=g.at[b, take, there * COLS : (there + rows) * COLS],
            dst_ref=g.at[p, take, here * COLS : (here + rows) * COLS],
            send_sem=h_send.at[n], recv_sem=h_recv.at[n],
            device_id=(jnp.clip(s - offset, 0, 31), k), device_id_type=MESH,
        )

    def halo_sends(p):
        for n, entry in enumerate(PARTS):
            if entry[0] == p:
                @pl.when((s - entry[1] >= 0) & (s - entry[1] <= 31))
                def _(n=n):
                    halo_copy(n).start()

    def halo_waits(p):
        for n, entry in enumerate(PARTS):
            if entry[0] == p:
                @pl.when((s + entry[1] >= 0) & (s + entry[1] <= 31))
                def _(n=n):
                    halo_copy(n).wait_recv()

    def halo_drain(p):
        for n, entry in enumerate(PARTS):
            if entry[0] == p:
                @pl.when((s - entry[1] >= 0) & (s - entry[1] <= 31))
                def _(n=n):
                    halo_copy(n).wait_send()

    def remote(src, dst, send, recv, target):
        return pltpu.make_async_remote_copy(
            src_ref=src, dst_ref=dst, send_sem=send, recv_sem=recv, device_id=target, device_id_type=MESH
        )

    def y_copy(p):
        return remote(g.at[p, own], g.at[p, own], y_send.at[p], y_recv.at[p], (s, k_pair))

    def pair_rows(first, count=2 * UNIT):
        return pl.ds(pl.multiple_of(first * UNIT, UNIT), count)

    def e_copies():
        return (
            remote(g.at[0, own], g.at[0, own], e_send.at[0], e_recv.at[0], (s, k_right)),
            remote(g.at[0, own], g.at[0, own], e_send.at[1], e_recv.at[1], (s, k_left)),
        )

    def x_copies(p):
        rows = pair_rows(k_pair, UNIT) if p == 0 else pair_rows(k_even)
        return (
            remote(g.at[p, rows], g.at[p, rows], x_send.at[p, 0], x_recv.at[p, 0], (s, k_right)),
            remote(g.at[p, rows], g.at[p, rows], x_send.at[p, 1], x_recv.at[p, 1], (s, k_left)),
        )

    def f_copies(p):
        from_left = pair_rows(lax.rem(k_even + 6, 8), UNIT)
        from_right = pair_rows(lax.rem(k_even + 2, 8) + 1, UNIT)
        return (
            remote(g.at[p, from_left], g.at[p, from_left], f_send.at[p, 0], f_recv.at[p, 0], (s, k_right)),
            remote(g.at[p, from_right], g.at[p, from_right], f_send.at[p, 1], f_recv.at[p, 1], (s, k_left)),
        )

    def stage_y(p):
        if PIECES[p][1] != 0:
            halo_waits(p)
        y_copy(p).start()

    def stage_x(p):
        y_copy(p).wait_recv()
        for copy in x_copies(p):
            copy.start()

    def stage_f(p):
        if p == 0:
            for copy in e_copies():
                copy.wait_recv()
        for copy in x_copies(p):
            copy.wait_recv()
        for copy in f_copies(p):
            copy.start()

    def stage_ready(p):
        if p in DIRECT:
            halo_waits(p)
        else:
            for copy in f_copies(p):
                copy.wait_recv()

    def transpose_kernels(p):
        b, i = PIECES[p]
        for j in range(3):
            wt[p, :, j * 256 : (j + 1) * 256] = w[b, (i + 1) * 3 + j].T

    def slot(p, j):
        return p if j is None else p + j

    def c_copy(p, j=None):
        src, dst = (part.at[p], r0.at[p]) if j is None else (part.at[p, j : j + 1], r0.at[p, j : j + 1])
        n = slot(p, j)
        return remote(src.at[:, :, :, 1 - core], dst, c_send.at[n], c_recv.at[n], (s + 1 - 2 * core, k))

    def v_copy(p, j=None):
        src, dst = (qs.at[p], ry.at[p]) if j is None else (qs.at[p, j], ry.at[p, j])
        n = slot(p, j)
        return remote(src, dst, v_send.at[n], v_recv.at[n], (lax.rem(s + 16, 32), k))

    def z_copy(p, d, j=None):
        z_to = lax.rem(zpos + d, 8)
        src, dst = sz.at[p, z_to], rz.at[p, d - 1]
        if j is not None:
            src, dst = src.at[j], dst.at[j]
        n = slot(p, j)
        return remote(src, dst, z_send.at[n], z_recv.at[n], (yl * 16 + z_to * 2 + core, k))

    def z_whole(p, j=None):
        src, dst = sz.at[p, 0:7], rz.at[p]
        if j is not None:
            src, dst = src.at[:, j], dst.at[:, j]
        n = slot(p, j)
        return remote(src, dst, z_send.at[n], z_recv.at[n], (lax.rem(s + 2, 32), k))

    def compute_kernels(p):
        b, i = PIECES[p]
        rate = RATES[b]

        lane = lax.broadcasted_iota(jnp.int32, (1, COLS), 1)
        keep_lo = (lane >= rate).astype(F32).astype(BF16)
        keep_hi = (lane < COLS - rate).astype(F32).astype(BF16)
        for y in range(STRIP):
            cols = slice(y * COLS, (y + 1) * COLS)
            value = g[p, :, cols]
            m3[0:256, cols] = pltpu.roll(value, COLS - rate, 1) * keep_hi
            m3[256:512, cols] = value
            m3[512:768, cols] = pltpu.roll(value, rate, 1) * keep_lo

        if p in SPLIT:
            for j in range(3):
                product = jnp.dot(m3[j * 256 : (j + 1) * 256, :], feat[...], preferred_element_type=F32)
                part[p, j] = product.reshape(2, 8, 2, 8, 256)
                c_copy(p, j).start()
        else:
            product = jnp.dot(m3[...], feat[...], preferred_element_type=F32)
            part[p] = product.reshape(3, 2, 8, 2, 8, 256)
            c_copy(p).start()

    def compute_input(p, first=False):
        for h in range(2):
            cols = slice(h * 1024, (h + 1) * 1024)
            product = jnp.dot(wt[p], m3[:, cols], preferred_element_type=F32)
            if first:
                acc[:, cols] = product
            else:
                acc[:, cols] += product

    def compute(p, first=False):
        compute_kernels(p)
        compute_input(p, first)

    def reduce_core(p, only=None):
        c_copy(p, only).wait_recv()
        for j in range(3) if only is None else (only,):
            qs[p, j] = part[p, j, 1 - yl, :, core] + r0[p, j, 1 - yl]
        v_copy(p, only).start()

    def reduce_y(p, only=None):
        v_copy(p, only).wait_recv()
        for j in range(3) if only is None else (only,):
            sz[p, :, j] = part[p, j, yl, :, core] + r0[p, j, yl] + ry[p, j]
        for d in range(1, 8):
            z_copy(p, d, only).start()

    def reduce_z(p):
        b, i = PIECES[p]
        for only in chunks(p):
            z_whole(p, only).wait_recv()
        total = sz[p, zpos]
        for d in range(7):
            total = total + rz[p, d]
        gw[b, 3 * (i + 1) : 3 * (i + 1) + 3] = total * grad_scale

    def own_first(_):
        for copy in e_copies():
            copy.start()

    def weights_in(_):
        w_copy.wait()
        feat_copy.wait()

    def split_core(p):
        for j in range(3):
            reduce_core(p, j)

    def split_y(p):
        for j in range(3):
            reduce_y(p, j)

    def write_input(_):
        for y in range(STRIP):
            gin[y] = acc[:, y * COLS : (y + 1) * COLS].astype(BF16).T

    steps = {
        "e": own_first, "y": stage_y, "h": halo_sends, "x": stage_x, "f": stage_f, "r": stage_ready,
        "w": weights_in, "t": transpose_kernels, "k": compute_kernels, "i": compute_input,
        "I": lambda p: compute_input(p, True), "c": reduce_core, "v": reduce_y, "z": reduce_z,
        "C": split_core, "V": split_y, "o": write_input,
    }
    for step in ORDER:
        steps[step[0]](int(step[1]))

    for copy in e_copies():
        copy.wait_send()
    for p in range(9):
        if PIECES[p][1] != 0:
            halo_drain(p)
        if p in RING:
            y_copy(p).wait_send()
            for copy in x_copies(p):
                copy.wait_send()
            for copy in f_copies(p):
                copy.wait_send()
        for j in chunks(p):
            c_copy(p, j).wait_send()
            v_copy(p, j).wait_send()
            z_whole(p, j).wait_send()


def shards(features, grad_out, pre_act, weights):
    dma = pltpu.SemaphoreType.DMA
    vmem = pl.BlockSpec(memory_space=pltpu.VMEM)
    return pl.pallas_call(
        kernel,
        out_shape=(
            jax.ShapeDtypeStruct((8, 256, 256), BF16),
            jax.ShapeDtypeStruct((3, 9, 8, 256), F32),
        ),
        in_specs=[pl.BlockSpec(memory_space=pl.ANY), vmem, vmem, pl.BlockSpec(memory_space=pl.ANY)],
        out_specs=(vmem, vmem),
        scratch_shapes=[
            pltpu.VMEM((2048, 256), BF16),
            pltpu.VMEM((3, 9, 256, 256), BF16),
            pltpu.VMEM((9, 256, 2048), BF16),
            pltpu.VMEM((768, 2048), BF16),
            pltpu.VMEM((9, 256, 768), BF16),
            pltpu.VMEM((256, 2048), F32),
            pltpu.VMEM((9, 3, 2, 8, 2, 8, 256), F32),
            pltpu.VMEM((9, 3, 2, 8, 8, 256), F32),
            pltpu.VMEM((9, 3, 8, 8, 256), F32),
            pltpu.VMEM((9, 3, 8, 8, 256), F32),
            pltpu.VMEM((9, 8, 3, 8, 256), F32),
            pltpu.VMEM((9, 7, 3, 8, 256), F32),
            dma((len(PARTS),)), dma((len(PARTS),)),
            dma((9,)), dma((9,)),
            dma((9, 2)), dma((9, 2)),
            dma((9, 2)), dma((9, 2)),
            dma((11,)), dma((11,)),
            dma((11,)), dma((11,)),
            dma((11,)), dma((11,)),
            dma((2,)), dma((2,)),
            pltpu.SemaphoreType.DMA,
            pltpu.SemaphoreType.DMA,
        ],
        compiler_params=pltpu.CompilerParams(
            collective_id=0, has_side_effects=True, vmem_limit_bytes=62 * 2**20
        ),
        cost_estimate=pl.CostEstimate(flops=14495514624, bytes_accessed=8 * 2**20, transcendentals=0),
    )(features.reshape(2048, 256), grad_out, pre_act, weights)


def solution(mesh):
    in_specs = (
        P("rows", None, "chan"),
        P(None, "rows", "chan", None),
        P(None, "rows", "chan", None),
        P(None, None, None, "chan"),
    )
    out_specs = (P("rows", None, "chan"), P(None, None, "rows", "chan"))
    return jax.shard_map(shards, mesh=mesh, in_specs=in_specs, out_specs=out_specs, check_vma=False)
```
